256 devices in a mesh: dp: 16 (over z_hi, x), section: 4 (over z_lo, core), tensor: 4 (over y).
Axes of the slice: x: 4, y: 4, z: 8 (z_hi: 4, z_lo: 2; z = z_hi * 2 + z_lo), core: 2. Of those that a mesh axis runs over, the one named last changes fastest.
Arguments:
- tiles: bfloat16 [768, 32, 3200], P(('dp', 'section'), None, 'tensor'), may hold values from -6 to 6
- ln_gain: float32 [3200], replicated, may hold values from 0.1 to 1.9
- w_fc1: bfloat16 [3200, 6400], P('section', 'tensor'), may hold values from -0.109375 to 0.109375
- w_fc2: bfloat16 [3200, 6400], P('section', 'tensor'), may hold values from -0.078125 to 0.078125
- tile_count: int32 [16, 4], P('dp', 'section'), may hold values from 1 to 12, 24 in all within a row
- embed_grad: bfloat16 [768, 32, 3200], P(('dp', 'section'), None, 'tensor'), may hold values from -6 to 6
Outputs:
- embeds: bfloat16 [768, 32, 3200], P(('dp', 'section'), None, 'tensor')
- grad_fc1: float32 [3200, 4, 1600], P('section', 'tensor', 'dp')
- grad_fc2: float32 [3200, 4, 1600], P('section', 'tensor', 'dp')
The draws below stay inside these ranges and needn't reach their ends.
Inputs may be any that keep to these rules, and one draw needn't show every extreme that they name: The counts of one row of tile_count add up to 24; the largest count of every row is 12.
All inputs are finite; a program needn't handle non-finite values. No bound on the sum of `tile_count` on one device may be relied on, other than what follows from the above.
Results may differ from the reference program's by a relative error of at most 0.022.
Values may be sent and summed in bfloat16 or wider, within the bound.
No kernel may reach another device: no remote copies, remote signals or barrier semaphores. Data moves between devices by JAX's collectives and lax.ppermute only.
A program may use at most 128 MiB of HBM per device.

```python
import math
import jax
import jax.numpy as jnp
import numpy as np
from jax import lax

D = 3200
FFW = 6400
MAXT = 12
SLOTS = 6
P_SIZE = 32
IMAGES = 64
N_DP = 16
N_SECTION = 4
N_TENSOR = 4


def block_scale(key, extent, split, smallest, high):
    def one(position, parts):
        steps = jax.random.uniform(jax.random.fold_in(jax.random.fold_in(key, 6), position), (parts,), jnp.float32, smallest / len(split), high / len(split))
        return jnp.repeat(jnp.exp(steps), extent[position] // parts).reshape((-1,) + (1,) * (len(extent) - position - 1))

    loudness = one(*split[0])
    for cut in split[1:]:
        loudness = loudness * one(*cut)
    return loudness


def split_up(count, total, bound, lean):
    loads = [(1 << 20) // math.isqrt(standing ** lean) + 1 for standing in range(2, count + 1)]
    surplus, counts = total - bound - (count - 1), [1] * (count - 1)
    while surplus > 0:
        candidates = [i for i in range(count - 1) if counts[i] < bound]
        pool, budget = sum([loads[i] for i in candidates]), surplus
        for i in candidates:
            more = min(bound - counts[i], max(1, budget * loads[i] // pool), surplus)
            counts[i] = counts[i] + more
            surplus = surplus - more
    return np.array([bound] + counts)


def ragged_sizes(stream_key, number_of, total, reach, lean):
    if number_of == 2:
        one = jax.random.randint(stream_key, (), max(1, total - reach), min(reach, total - 1) + 1)
        return jnp.stack([one, total - one])
    lengths = jnp.asarray(split_up(number_of, total, reach, lean), jnp.int32)
    couples = (number_of - 1) // 2
    source_of, receiver = lengths[1:1 + 2 * couples:2], lengths[2:2 + 2 * couples:2]
    slack = jnp.minimum(source_of - 1, reach - receiver)
    shifted = jax.random.randint(jax.random.fold_in(stream_key, 1), (couples,), 0, 1 << 20) % (slack + 1)
    lengths = lengths.at[1:1 + 2 * couples:2].set(source_of - shifted).at[2:2 + 2 * couples:2].set(receiver + shifted)
    return lengths[jax.random.permutation(jax.random.fold_in(stream_key, 2), number_of)]


def normal_values(own_key, shape, scale, limit, cuts=(), kind=jnp.bfloat16):
    drawn = jax.random.normal(own_key, shape, jnp.float32) * scale
    if len(cuts) > 0:
        drawn = block_scale(own_key, shape, cuts, -0.22, 0.18) * drawn
    return jnp.clip(drawn, min=-limit, max=limit).astype(kind)


def setup_inputs(seed: int = 0) -> dict:
    streams_of = jax.random.split(jax.random.key(seed), 7)
    return {
        "tiles": normal_values(streams_of[0], (IMAGES * MAXT, P_SIZE, D), 1.0, 6.0, ((0, 64), (2, 4))),
        "ln_gain": jnp.clip(1.0 + 0.18 * jax.random.normal(streams_of[1], (D,), jnp.float32), 0.1, 1.9),
        "w_fc1": normal_values(streams_of[2], (D, FFW), D ** -0.5, 0.109375, ((0, 4), (1, 4))),
        "w_fc2": normal_values(streams_of[3], (D, FFW), FFW ** -0.5, 0.078125, ((0, 4), (1, 4))),
        "tile_count": jax.vmap(lambda own: ragged_sizes(own, N_SECTION, SLOTS * N_SECTION, MAXT, 2))(jax.random.split(streams_of[4], N_DP)).reshape((N_DP, N_SECTION)).astype(jnp.int32),
        "embed_grad": normal_values(streams_of[5], (IMAGES * MAXT, P_SIZE, D), 1.0, 6.0, ((0, 64), (2, 4))),
    }


epsilon = 1e-06

def gelu_slope(values):
    normal_cdf = 0.5 * (1.0 + lax.erf(values * 0.7071067811865476))
    return normal_cdf + values * jnp.exp(-0.5 * values * values) * 0.3989422804014327

def rms_norm(values, ln_gain):
    square_mean = lax.optimization_barrier(jnp.mean(values * values, axis=-1, keepdims=True))
    return (values * lax.rsqrt(square_mean + epsilon) * ln_gain).astype(jnp.bfloat16)

def reference(tiles, ln_gain, w_fc1, w_fc2, tile_count, embed_grad):
    live_tile = jnp.arange(MAXT)[None, :] < tile_count.reshape(-1, 1)
    live_rows = jnp.repeat(live_tile.reshape(-1), P_SIZE)[:, None]
    inputs = tiles.reshape(-1, D).astype(jnp.float32)
    normed = rms_norm(inputs, ln_gain)
    before = jnp.dot(normed, w_fc1, preferred_element_type=jnp.float32)
    hidden = jax.nn.gelu(before, approximate=False).astype(jnp.bfloat16)
    mixed = lax.dot_general(hidden, w_fc2, (((1,), (1,)), ((), ())), preferred_element_type=jnp.float32)
    embeds = jnp.where(live_rows, inputs + mixed, 0.0).astype(jnp.bfloat16).reshape(tiles.shape)
    cotangent = jnp.where(live_rows, embed_grad.reshape(-1, D), jnp.zeros((), jnp.bfloat16))
    slope_in = jnp.dot(cotangent, w_fc2, preferred_element_type=jnp.float32)
    d_before = (slope_in * gelu_slope(before)).astype(jnp.bfloat16)
    group_rows = N_SECTION * MAXT * P_SIZE

    def add_replica(replica, totals):
        begin = (replica * group_rows).astype(jnp.int32)
        normed_part = lax.dynamic_slice_in_dim(normed, begin, group_rows, 0)
        slope_part = lax.dynamic_slice_in_dim(d_before, begin, group_rows, 0)
        grad_part = lax.dynamic_slice_in_dim(cotangent, begin, group_rows, 0)
        hidden_part = lax.dynamic_slice_in_dim(hidden, begin, group_rows, 0)
        term_fc1 = lax.dot_general(normed_part, slope_part, (((0,), (0,)), ((), ())), preferred_element_type=jnp.float32)
        term_fc2 = lax.dot_general(grad_part, hidden_part, (((0,), (0,)), ((), ())), preferred_element_type=jnp.float32)
        term_fc1 = lax.optimization_barrier(term_fc1.astype(jnp.bfloat16)).astype(jnp.float32)
        term_fc2 = lax.optimization_barrier(term_fc2.astype(jnp.bfloat16)).astype(jnp.float32)
        return (totals[0] + term_fc1, totals[1] + term_fc2)
    zero_grad = jnp.zeros((D, FFW), jnp.float32)
    grad_fc1, grad_fc2 = lax.fori_loop(0, N_DP, add_replica, (zero_grad, zero_grad))
    return (embeds, grad_fc1.reshape(D, N_TENSOR, FFW // N_TENSOR), grad_fc2.reshape(D, N_TENSOR, FFW // N_TENSOR))
```

```python
import functools

import jax
import jax.numpy as jnp
from jax import lax
from jax.experimental import pallas as pl
from jax.experimental.pallas import tpu as pltpu
from jax.sharding import PartitionSpec as P

epsilon = 1e-06
F32 = jnp.float32
BF16 = jnp.bfloat16
PEERS = 4
TARGET_SLOTS = 6


def gelu_slope(values):
    normal_cdf = 0.5 * (1.0 + lax.erf(values * 0.7071067811865476))
    return normal_cdf + values * jnp.exp(-0.5 * values * values) * 0.3989422804014327


def section_swap(x, mask):
    return lax.ppermute(x, "section", [(s, s ^ mask) for s in range(PEERS)])


def tensor_ring(x, step):
    return lax.ppermute(x, "tensor", [(t, (t + step) % PEERS) for t in range(PEERS)])


def x_ring(x, step, replicas):
    pairs = [(d, d - d % PEERS + (d % PEERS + step) % PEERS) for d in range(replicas)]
    return lax.ppermute(x, "dp", pairs)


def z_ring(x, step, replicas):
    pairs = [(d, (d + step * PEERS) % replicas) for d in range(replicas)]
    return lax.ppermute(x, "dp", pairs)


def dispatch(x, step):
    pairs = [(i * PEERS + f, f * PEERS + (i + step) % PEERS) for i in range(PEERS) for f in range(PEERS)]
    return lax.ppermute(x, ("section", "tensor"), pairs)


def give_back(x, step):
    pairs = [(f * PEERS + (i + step) % PEERS, i * PEERS + f) for i in range(PEERS) for f in range(PEERS)]
    return lax.ppermute(x, ("section", "tensor"), pairs)


def compact_kernel(places, got_0, got_1, got_2, got_3, out):
    for k, got in enumerate((got_0, got_1, got_2, got_3)):
        for p in range(got.shape[0]):

            @pl.when(p < places[PEERS + k])
            def _():
                out[places[k] + p] = got[p]


def compact(places, got):
    shape = (TARGET_SLOTS,) + got[0].shape[1:]
    return pl.pallas_call(
        compact_kernel,
        out_shape=jax.ShapeDtypeStruct(shape, got[0].dtype),
        in_specs=[pl.BlockSpec(memory_space=pltpu.SMEM)] + [pl.BlockSpec(memory_space=pltpu.VMEM)] * 4,
        out_specs=pl.BlockSpec(memory_space=pltpu.VMEM),
        cost_estimate=pl.CostEstimate(flops=0, bytes_accessed=1000000, transcendentals=0),
    )(places, *got)


def pick(values, index):
    return sum(jnp.where(index == i, values[i], 0) for i in range(len(values)))


def body(tiles, ln_gain, w_fc1, w_fc2, tile_count, embed_grad):
    replicas = lax.axis_size("dp")
    section = lax.axis_index("section")
    tensor = lax.axis_index("tensor")
    replica = lax.axis_index("dp")
    core = section % 2
    max_tiles, tile_rows, width_part = tiles.shape
    width = ln_gain.shape[0]
    hidden_part = w_fc1.shape[1]
    columns = hidden_part // replicas
    groups = max_tiles // PEERS
    half = TARGET_SLOTS * tile_rows * 2
    chunk = TARGET_SLOTS * tile_rows

    own_count = tile_count.reshape(())
    by_mask = [own_count] + [section_swap(own_count, m) for m in (1, 2, 3)]
    counts = [pick(by_mask, section ^ i) for i in range(PEERS)]
    offsets = [jnp.zeros((), jnp.int32)]
    for i in range(PEERS - 1):
        offsets.append(offsets[-1] + counts[i])
    own_offset = pick(offsets, section)

    values = tiles.astype(F32)
    squares = jnp.sum(values * values, axis=-1)
    squares = squares + sum(tensor_ring(squares, k) for k in (1, 2, 3))
    gain = lax.dynamic_index_in_dim(ln_gain.reshape(PEERS, width_part), tensor, 0, keepdims=False)
    scale = lax.rsqrt(squares / width + epsilon)
    normed = (values * scale[:, :, None] * gain).astype(BF16)

    def send(x):
        x = x.reshape(groups, PEERS, tile_rows, width_part)
        got = []
        for k in range(PEERS):
            first = (section + k - own_offset) % PEERS
            got.append(dispatch(lax.dynamic_index_in_dim(x, first, 1, keepdims=False), k))
        return got

    bases, lives = [], []
    for k in range(PEERS):
        source = (tensor - k) % PEERS
        source_offset = pick(offsets, source)
        first = (tensor - source_offset) % PEERS
        bases.append((source_offset + first) // PEERS)
        lives.append(jnp.clip((pick(counts, source) - first + PEERS - 1) // PEERS, 0, groups))
    places = jnp.stack(bases + lives).astype(jnp.int32)

    def collect(x):
        own = compact(places, send(x)).reshape(chunk, width_part)
        pieces = [own] + [tensor_ring(own, k) for k in (1, 2, 3)]
        whole = jnp.concatenate(pieces, axis=0)
        mine = lax.dynamic_slice_in_dim(whole, core * half, half, 0)
        other = lax.dynamic_slice_in_dim(whole, (1 - core) * half, half, 0)
        return mine, other

    def in_x_order(w):
        w = w.reshape(width_part, replicas // PEERS, PEERS, columns)
        return w.transpose(0, 2, 1, 3).reshape(width_part, hidden_part)

    up = in_x_order(w_fc1)
    down = in_x_order(w_fc2)
    norm_mine, norm_other = collect(normed)
    grad_mine, grad_other = collect(embed_grad)

    def project(mine, other, w):
        away = jnp.dot(other, w, preferred_element_type=F32).astype(BF16)
        away = section_swap(away, 1)
        chip = jnp.dot(mine, w, preferred_element_type=F32) + away.astype(F32)
        chip = chip.astype(BF16)
        return chip.astype(F32) + section_swap(chip, 2).astype(F32)

    before = project(norm_mine, norm_other, up)
    hidden_mine = jax.nn.gelu(before, approximate=False).astype(BF16)
    hidden = jnp.concatenate([hidden_mine, section_swap(hidden_mine, 1)], axis=0)
    slope_in = project(grad_mine, grad_other, down)
    slope_mine = (slope_in * gelu_slope(before)).astype(BF16)
    slope = jnp.concatenate([slope_mine, section_swap(slope_mine, 1)], axis=0)

    partial = lax.dot_general(hidden, down, (((1,), (1,)), ((), ())), preferred_element_type=F32)
    partial = partial.astype(BF16)
    terms = []
    for k in range(PEERS):
        begin = (k * chunk + core * half) % (2 * half)
        piece = lax.dynamic_slice_in_dim(partial, begin, chunk, 0)
        terms.append(piece if k == 0 else tensor_ring(piece, -k))
    mixed = sum(term.astype(F32) for term in terms).astype(BF16)
    mixed = mixed.reshape(TARGET_SLOTS, tile_rows, width_part)
    mixed = jnp.pad(mixed, ((0, groups), (0, 0), (0, 0)))
    back = []
    for k in range(PEERS):
        back.append(give_back(lax.dynamic_slice_in_dim(mixed, bases[k], groups, 0), k))
    rows = []
    for j in range(PEERS):
        step = (own_offset + j - section) % PEERS
        rows.append(sum(jnp.where(step == k, back[k].astype(F32), 0.0) for k in range(PEERS)))
    back = jnp.stack(rows, axis=1).reshape(tiles.shape)
    live = jnp.arange(max_tiles, dtype=jnp.int32)[:, None, None] < own_count
    embeds = jnp.where(live, values + back, 0.0).astype(BF16)

    def reduce(left, right):
        term = lax.dot_general(left, right, (((0,), (0,)), ((), ())), preferred_element_type=F32)
        term = term.astype(BF16)
        rows = hidden_part // PEERS
        total = None
        for k in range(PEERS):
            piece = lax.dynamic_slice_in_dim(term, (replica + k) % PEERS * rows, rows, 0)
            piece = (piece if k == 0 else x_ring(piece, k, replicas)).astype(F32)
            total = piece if total is None else total + piece
        layers = replicas // PEERS
        term = total.astype(BF16).reshape(layers, columns, width_part)
        total = None
        for k in range(layers):
            piece = lax.dynamic_index_in_dim(term, (replica // PEERS + k) % layers, 0, keepdims=False)
            piece = (piece if k == 0 else z_ring(piece, k, replicas)).astype(F32)
            total = piece if total is None else total + piece
        return total.T.reshape(width_part, 1, columns)

    grad_fc2 = reduce(hidden, jnp.concatenate([grad_mine, grad_other], axis=0))
    grad_fc1 = reduce(slope, jnp.concatenate([norm_mine, norm_other], axis=0))
    return (embeds, grad_fc1, grad_fc2)


def solution(mesh):
    placed = (
        P(("dp", "section"), None, "tensor"),
        P(),
        P("section", "tensor"),
        P("section", "tensor"),
        P("dp", "section"),
        P(("dp", "section"), None, "tensor"),
    )
    return jax.shard_map(
        body,
        mesh=mesh,
        in_specs=placed,
        out_specs=(
            P(("dp", "section"), None, "tensor"),
            P("section", "tensor", "dp"),
            P("section", "tensor", "dp"),
        ),
        check_vma=False,
    )
```

```python
import functools

import jax
import jax.numpy as jnp
import numpy as np
from jax import lax
from jax.experimental import pallas as pl
from jax.experimental.pallas import tpu as pltpu
from jax.sharding import PartitionSpec as P

epsilon = 1e-06
F32 = jnp.float32
BF16 = jnp.bfloat16
PEERS = 4
TARGET_SLOTS = 6
CUTS = (0, 96, 200)
VMEM = pl.BlockSpec(memory_space=pltpu.VMEM)
SMEM = pl.BlockSpec(memory_space=pltpu.SMEM)


def gelu_slope(values):
    normal_cdf = 0.5 * (1.0 + lax.erf(values * 0.7071067811865476))
    return normal_cdf + values * jnp.exp(-0.5 * values * values) * 0.3989422804014327


def section_swap(x, mask):
    return lax.ppermute(x, "section", [(s, s ^ mask) for s in range(PEERS)])


def tensor_ring(x, step):
    return lax.ppermute(x, "tensor", [(t, (t + step) % PEERS) for t in range(PEERS)])


def x_ring(x, step, replicas):
    pairs = [(d, d - d % PEERS + (d % PEERS + step) % PEERS) for d in range(replicas)]
    return lax.ppermute(x, "dp", pairs)


def z_ring(x, step, replicas):
    pairs = [(d, (d + step * PEERS) % replicas) for d in range(replicas)]
    return lax.ppermute(x, "dp", pairs)


def dispatch(x, step):
    pairs = [(i * PEERS + f, f * PEERS + (i + step) % PEERS) for i in range(PEERS) for f in range(PEERS)]
    return lax.ppermute(x, ("section", "tensor"), pairs)


def give_back(x, step):
    pairs = [(f * PEERS + (i + step) % PEERS, i * PEERS + f) for i in range(PEERS) for f in range(PEERS)]
    return lax.ppermute(x, ("section", "tensor"), pairs)


def cost(flops, moved):
    return pl.CostEstimate(flops=flops, bytes_accessed=moved, transcendentals=0)


def after(x, *others):
    return lax.optimization_barrier((x,) + others)[0]


def choose(values, index):
    chosen = values[0]
    for i in range(1, len(values)):
        chosen = jnp.where(index == i, values[i], chosen)
    return chosen


def read_counts(info):
    section = info[0]
    counts = [choose([info[2 + m] for m in range(PEERS)], section ^ i) for i in range(PEERS)]
    offsets = [jnp.int32(0)]
    for i in range(PEERS - 1):
        offsets.append(offsets[-1] + counts[i])
    return counts, offsets


def first_of(info, offsets, k):
    section = info[0]
    return (section + k - choose(offsets, section)) & (PEERS - 1)


def plan_kernel(groups, info, out):
    counts, offsets = read_counts(info)
    tensor = info[1]
    out[3 * PEERS] = info[2]
    for k in range(PEERS):
        out[k] = first_of(info, offsets, k)
        source = (tensor - k) & (PEERS - 1)
        offset = choose(offsets, source)
        first = (tensor - offset) & (PEERS - 1)
        out[PEERS + k] = (offset + first) >> 2
        live = (choose(counts, source) - first + PEERS - 1) >> 2
        out[2 * PEERS + k] = jnp.minimum(jnp.maximum(live, 0), groups)


def pack_kernel(info, rows, *sends):
    _, offsets = read_counts(info)
    for k in range(PEERS):
        first = first_of(info, offsets, k)
        for p in range(sends[k].shape[0]):
            sends[k][p] = rows[first + PEERS * p]


def compact_kernel(plan, g0, g1, g2, g3, out):
    for k, got in enumerate((g0, g1, g2, g3)):
        for p in range(got.shape[0]):

            @pl.when(p < plan[2 * PEERS + k])
            def _():
                out[plan[PEERS + k] + p] = got[p]


def expand_kernel(plan, m0, m1, m2, m3, *outs):
    for k in range(PEERS):
        for p in range(outs[k].shape[0]):
            slot = jnp.minimum(plan[PEERS + k] + p, TARGET_SLOTS - 1)
            total = m0[slot].astype(F32) + m1[slot].astype(F32)
            total = total + m2[slot].astype(F32) + m3[slot].astype(F32)
            outs[k][p] = total.astype(BF16)


def finish_kernel(plan, tiles, b0, b1, b2, b3, out):
    for k, back in enumerate((b0, b1, b2, b3)):
        for p in range(back.shape[0]):
            j = plan[k] + PEERS * p
            total = (tiles[j].astype(F32) + back[p].astype(F32)).astype(BF16)
            out[j] = jnp.where(j < plan[3 * PEERS], total, jnp.zeros_like(total))


def local(kernel, out_shape, scalars, arrays):
    single = not isinstance(out_shape, list)
    return pl.pallas_call(
        kernel,
        out_shape=out_shape,
        in_specs=[SMEM] * len(scalars) + [VMEM] * len(arrays),
        out_specs=VMEM if single else [VMEM] * len(out_shape),
        cost_estimate=cost(0, 2000000),
    )(*scalars, *arrays)


def column_picks(hidden, columns, layers):
    share = columns // 2
    order = []
    for half in range(2):
        for low, high in zip(CUTS[:-1], CUTS[1:]):
            for x in range(PEERS):
                for spot in range(low, high):
                    layer, rest = spot // share, spot % share
                    order.append(layer * PEERS * columns + x * columns + half * share + rest)
    picks = np.zeros((hidden, hidden), np.float32)
    picks[np.arange(hidden), np.array(order)] = 1.0
    return picks.reshape(2, hidden // 2, hidden).astype(jnp.bfloat16)


def body(tiles, ln_gain, w_fc1, w_fc2, tile_count, embed_grad):
    replicas = lax.axis_size("dp")
    section = lax.axis_index("section")
    tensor = lax.axis_index("tensor")
    replica = lax.axis_index("dp")
    core = section % 2
    max_tiles, tile_rows, width_part = tiles.shape
    width = ln_gain.shape[0]
    hidden_part = w_fc1.shape[1]
    columns = hidden_part // replicas
    share = columns // 2
    layers = replicas // PEERS
    groups = max_tiles // PEERS
    chunk = TARGET_SLOTS * tile_rows
    rows = PEERS * chunk
    block = jax.ShapeDtypeStruct((groups, tile_rows, width_part), BF16)
    slots = jax.ShapeDtypeStruct((TARGET_SLOTS, tile_rows, width_part), BF16)
    spans = [(low * PEERS, high * PEERS) for low, high in zip(CUTS[:-1], CUTS[1:])]
    last = []

    def turn(x):
        return after(x, last[-1]) if last else x

    def done(x):
        last.append(x)
        return x

    own_count = tile_count.reshape(1)
    place = jnp.stack([section, tensor]).astype(jnp.int32)
    all_counts = [own_count] + [section_swap(own_count, m) for m in (1, 2, 3)]
    info = jnp.concatenate([place] + all_counts)
    gains = ln_gain.reshape(PEERS, width_part)
    gain_mine = lax.dynamic_index_in_dim(gains, section, 0)
    gain_away = lax.dynamic_index_in_dim(gains, section ^ 1, 0)

    def send(x):
        sends = local(pack_kernel, [block] * PEERS, [info], [turn(x)])
        done(sends[0])
        return [dispatch(sends[k], k) for k in range(PEERS)]

    def compact(got):
        own = local(compact_kernel, slots, [plan], [turn(got[0]), *got[1:]])
        own = done(own.reshape(chunk, width_part))
        near = [tensor_ring(own, k) for k in (1, 3)]
        return [own, near[0], tensor_ring(own, 2), near[1]]

    def join(pieces):
        return done(jnp.concatenate([turn(pieces[0])] + pieces[1:], axis=0))

    def reordered(w, half, factor=None):
        pick = lax.dynamic_index_in_dim(picks, half, 0, keepdims=False)
        part = lax.dot_general(pick, turn(w), (((1,), (1,)), ((), ())), preferred_element_type=F32)
        if factor is not None:
            part = part * factor
        return done(part.astype(BF16))

    contract = (((1,), (1,)), ((), ()))

    def project(w_mine, w_away, rows_mine, rows_away):
        firsts = []
        for a, b in spans:
            firsts.append(lax.dot_general(w_mine[a:b], turn(rows_mine), contract, preferred_element_type=F32))
        terms = []
        for (a, b), first in zip(spans, firsts):
            second = lax.dot_general(w_away[a:b], turn(rows_away), contract, preferred_element_type=F32)
            terms.append(done((first + second).astype(BF16)))
        return [(term, section_swap(term, 2)) for term in terms]

    def over_x(left, right, factor=None):
        term = jnp.dot(left, right, preferred_element_type=F32)
        if factor is not None:
            term = term * factor
        term = done(term.astype(BF16))
        count = term.shape[0] // PEERS
        got = {}
        for k in (0, 1, 3, 2):
            piece = lax.dynamic_slice_in_dim(term, (replica + k) % PEERS * count, count, 0)
            got[k] = piece if k == 0 else x_ring(piece, k, replicas)
        return [got[k] for k in range(PEERS)]

    def over_z(parts):
        sums = []
        for part in parts:
            part = [turn(part[0])] + part[1:]
            sums.append(done(sum(piece.astype(F32) for piece in part).astype(BF16)))
        term = jnp.concatenate(sums, axis=0).reshape(layers, share, 2 * width_part)
        got = []
        for k in range(layers):
            piece = lax.dynamic_index_in_dim(term, (replica // PEERS + k) % layers, 0, keepdims=False)
            got.append(piece if k == 0 else z_ring(piece, k, replicas))
        return got

    def place_result(got):
        total = sum(piece.astype(F32) for piece in got)
        mine, away = total[:, :width_part], total[:, width_part:]
        away = section_swap(away, 1)
        whole = jnp.where(core == 0, jnp.concatenate([mine, away]), jnp.concatenate([away, mine]))
        return whole.T.reshape(width_part, 1, columns)

    tiles_got = send(tiles)
    grads_got = send(embed_grad)
    plan = pl.pallas_call(
        functools.partial(plan_kernel, groups),
        out_shape=jax.ShapeDtypeStruct((16,), jnp.int32),
        in_specs=[SMEM],
        out_specs=SMEM,
    )(turn(info))
    picks = jnp.asarray(column_picks(hidden_part, columns, layers))
    up_away = section_swap(reordered(w_fc1, 1 - core, gain_mine), 1)
    norm_pieces = compact(tiles_got)
    up_mine = reordered(w_fc1, core, gain_mine)
    grad_pieces = compact(grads_got)
    norm_mine = join(norm_pieces)
    norm_away = section_swap(norm_mine, 1)
    sums = project(up_mine, up_away, norm_mine, norm_away)

    squares = sum(
        jnp.sum(jnp.square(turn(x).astype(F32)), axis=1).reshape(1, rows) for x in (norm_mine, norm_away)
    )
    squares = done(squares)
    squares = squares + section_swap(squares, 2)
    scale = lax.rsqrt(squares / width + epsilon)
    down_away = section_swap(reordered(w_fc2, 1 - core), 1)
    grad_mine = join(grad_pieces)
    grad_away = section_swap(grad_mine, 1)
    down_mine = reordered(w_fc2, core)

    def before_of(c):
        one, two = sums[c]
        return (one.astype(F32) + turn(two).astype(F32)) * scale

    def activate(c):
        return done(jax.nn.gelu(before_of(c), approximate=False).astype(BF16))

    def slope_of(c):
        one, two = slopes_in[c]
        slope = (one.astype(F32) + two.astype(F32)) * gelu_slope(before_of(c)) * scale
        return done(slope.astype(BF16))

    norm_rows = jnp.concatenate([norm_mine, norm_away], axis=1)
    grad_rows = jnp.concatenate([turn(grad_mine), grad_away], axis=1)
    factor = jnp.concatenate([gain_mine, gain_away], axis=1)
    hidden = [activate(0)]
    parts_fc2 = [over_x(hidden[0], grad_rows)]
    slopes_in = project(down_mine, down_away, grad_mine, grad_away)
    for c in range(1, len(spans)):
        hidden.append(activate(c))
        parts_fc2.append(over_x(hidden[c], grad_rows))

    def mix(w):
        return sum(
            lax.dot_general(turn(h), w[a:b], (((0,), (0,)), ((), ())), preferred_element_type=F32)
            for h, (a, b) in zip(hidden, spans)
        )

    mix_away = section_swap(done(mix(down_away).astype(BF16)), 1)
    mixed = mix(down_mine)
    done(mixed)
    parts_fc1 = [over_x(slope_of(0), norm_rows, factor)]
    mixed = done((turn(mixed) + mix_away.astype(F32)).astype(BF16))
    terms = []
    for k in range(PEERS):
        piece = mixed[k * chunk : (k + 1) * chunk]
        piece = piece if k == 0 else tensor_ring(piece, -k)
        terms.append(piece.reshape(slots.shape))
    for c in range(1, len(spans)):
        parts_fc1.append(over_x(slope_of(c), norm_rows, factor))
    spread = local(expand_kernel, [block] * PEERS, [plan], [turn(terms[0]), *terms[1:]])
    done(spread[0])
    back = [give_back(spread[k], k) for k in range(PEERS)]
    got_fc2 = over_z(parts_fc2)
    embeds = local(
        finish_kernel, jax.ShapeDtypeStruct(tiles.shape, BF16), [plan], [turn(tiles), *back]
    )
    got_fc1 = over_z(parts_fc1)
    return (embeds, place_result(got_fc1), place_result(got_fc2))


def solution(mesh):
    placed = (
        P(("dp", "section"), None, "tensor"),
        P(),
        P("section", "tensor"),
        P("section", "tensor"),
        P("dp", "section"),
        P(("dp", "section"), None, "tensor"),
    )
    return jax.shard_map(
        body,
        mesh=mesh,
        in_specs=placed,
        out_specs=(
            P(("dp", "section"), None, "tensor"),
            P("section", "tensor", "dp"),
            P("section", "tensor", "dp"),
        ),
        check_vma=False,
    )
```

```python
import functools

import jax
import jax.numpy as jnp
import numpy as np
from jax import lax
from jax.experimental import pallas as pl
from jax.experimental.pallas import tpu as pltpu
from jax.sharding import PartitionSpec as P

epsilon = 1e-06
F32 = jnp.float32
BF16 = jnp.bfloat16
PEERS = 4
TARGET_SLOTS = 6
TILE = 16
CHUNKS = ((0, 32, 32), (32, 50, 20))
VMEM = pl.BlockSpec(memory_space=pltpu.VMEM)
SMEM = pl.BlockSpec(memory_space=pltpu.SMEM)


def gelu_slope(values):
    normal_cdf = 0.5 * (1.0 + lax.erf(values * 0.7071067811865476))
    return normal_cdf + values * jnp.exp(-0.5 * values * values) * 0.3989422804014327


def section_swap(x, mask):
    return lax.ppermute(x, "section", [(s, s ^ mask) for s in range(PEERS)])


def tensor_ring(x, step):
    return lax.ppermute(x, "tensor", [(t, (t + step) % PEERS) for t in range(PEERS)])


def x_ring(x, step, replicas):
    pairs = [(d, d - d % PEERS + (d % PEERS + step) % PEERS) for d in range(replicas)]
    return lax.ppermute(x, "dp", pairs)


def z_ring(x, step, replicas):
    pairs = [(d, (d + step * PEERS) % replicas) for d in range(replicas)]
    return lax.ppermute(x, "dp", pairs)


def dispatch(x, step):
    pairs = [(i * PEERS + f, f * PEERS + (i + step) % PEERS) for i in range(PEERS) for f in range(PEERS)]
    return lax.ppermute(x, ("section", "tensor"), pairs)


def give_back(x, step):
    pairs = [(f * PEERS + (i + step) % PEERS, i * PEERS + f) for i in range(PEERS) for f in range(PEERS)]
    return lax.ppermute(x, ("section", "tensor"), pairs)


def cost(flops, moved):
    return pl.CostEstimate(flops=flops, bytes_accessed=moved, transcendentals=0)


def after(x, *others):
    return lax.optimization_barrier((x,) + others)[0]


def choose(values, index):
    chosen = values[0]
    for i in range(1, len(values)):
        chosen = jnp.where(index == i, values[i], chosen)
    return chosen


def read_counts(info):
    section = info[0]
    counts = [choose([info[2 + m] for m in range(PEERS)], section ^ i) for i in range(PEERS)]
    offsets = [jnp.int32(0)]
    for i in range(PEERS - 1):
        offsets.append(offsets[-1] + counts[i])
    return counts, offsets


def first_of(info, offsets, k):
    section = info[0]
    return (section + k - choose(offsets, section)) & (PEERS - 1)


def plan_kernel(groups, info, out):
    counts, offsets = read_counts(info)
    tensor = info[1]
    out[3 * PEERS] = info[2]
    for k in range(PEERS):
        out[k] = first_of(info, offsets, k)
        source = (tensor - k) & (PEERS - 1)
        offset = choose(offsets, source)
        first = (tensor - offset) & (PEERS - 1)
        out[PEERS + k] = (offset + first) >> 2
        live = (choose(counts, source) - first + PEERS - 1) >> 2
        out[2 * PEERS + k] = jnp.minimum(jnp.maximum(live, 0), groups)


def pack_kernel(info, tiles, grads, *sends):
    _, offsets = read_counts(info)
    for k in range(PEERS):
        first = first_of(info, offsets, k)
        for p in range(sends[k].shape[1]):
            sends[k][0, p] = tiles[first + PEERS * p]
            sends[k][1, p] = grads[first + PEERS * p]


def compact_kernel(plan, g0, g1, g2, g3, tiles, grads):
    for k, got in enumerate((g0, g1, g2, g3)):
        for p in range(got.shape[1]):

            @pl.when(p < plan[2 * PEERS + k])
            def _():
                slot = plan[PEERS + k] + p
                tiles[slot] = got[0, p]
                grads[slot] = got[1, p]


def join_kernel(place, p0, p1, p2, p3, out):
    size = p0.shape[0]
    for k, piece in enumerate((p0, p1, p2, p3)):
        out[pl.ds(((place[1] - k) & (PEERS - 1)) * size, size)] = piece[...]


def expand_kernel(plan, mixed, *outs):
    for k in range(PEERS):
        for p in range(outs[k].shape[0]):
            slot = jnp.minimum(plan[PEERS + k] + p, TARGET_SLOTS - 1)
            total = mixed[0, slot].astype(F32) + mixed[1, slot].astype(F32)
            total = total + mixed[2, slot].astype(F32) + mixed[3, slot].astype(F32)
            outs[k][p] = total.astype(BF16)


def finish_kernel(plan, tiles, b0, b1, b2, b3, out):
    for k, back in enumerate((b0, b1, b2, b3)):
        for p in range(back.shape[0]):
            j = plan[k] + PEERS * p
            total = (tiles[j].astype(F32) + back[p].astype(F32)).astype(BF16)
            out[j] = jnp.where(j < plan[3 * PEERS], total, jnp.zeros_like(total))


def dot_rows(left, right, left_axis, right_axis):
    return lax.dot_general(left, right, (((left_axis,), (right_axis,)), ((), ())), preferred_element_type=F32)


def flat(ref):
    return ref[...].reshape(ref.shape[0] * ref.shape[1], ref.shape[2])


def reorder_kernel(half, pick, w, *rest):
    factor, out = rest if len(rest) == 2 else (None, rest[0])
    part = dot_rows(pick[0], w[...], 1, 1)
    if factor is not None:
        part = part * factor[...]
    out[...] = part.astype(BF16).reshape(out.shape)


def row_squares(rows):
    values = flat(rows).astype(F32)
    values = values * values
    high = values.astype(BF16)
    low = (values - high.astype(F32)).astype(BF16)
    ones = jnp.ones((TILE, values.shape[1]), BF16)
    return dot_rows(ones, high, 1, 1) + dot_rows(ones, low, 1, 1)


def project_kernel(begin, count, w_mine, w_away, rows_mine, rows_away, out):
    step = count // PEERS
    if out.shape[0] > count:
        squares = row_squares(rows_mine) + row_squares(rows_away)
        high = squares.astype(BF16)
        rest = squares - high.astype(F32)
        middle = rest.astype(BF16)
        low = (rest - middle.astype(F32)).astype(BF16)
        spot = lax.broadcasted_iota(jnp.int32, squares.shape, 0)
        part = jnp.where(spot == 0, high.astype(F32), jnp.where(spot == 1, middle.astype(F32), low.astype(F32)))
        out[count:, :] = jnp.where(spot < 3, part, 0.0).astype(BF16)

    def piece(i, carry):
        at = pl.ds((begin + i * step) // TILE, step // TILE)
        mine = w_mine[at].reshape(step, w_mine.shape[2])
        away = w_away[at].reshape(step, w_away.shape[2])
        total = dot_rows(mine, flat(rows_mine), 1, 1) + dot_rows(away, flat(rows_away), 1, 1)
        out[pl.ds(pl.multiple_of(i * step, TILE), step), :] = total.astype(BF16)
        return carry

    lax.fori_loop(0, PEERS, piece, 0)


def scale_of(width, one, two, count):
    if one.shape[0] > count:
        one, two = one.at[pl.ds(count, TILE), :], two.at[pl.ds(count, TILE), :]
    both = one[...].astype(F32) + two[...].astype(F32)
    return lax.rsqrt(jnp.sum(both, axis=0, keepdims=True) * (1.0 / width) + epsilon)


def fc2_kernel(features, x, one, two, tail_one, tail_two, rows_mine, rows_away, hidden, *terms):
    step = terms[0].shape[0]
    width = rows_mine.shape[2]
    scale = scale_of(features, tail_one, tail_two, PEERS * step)
    for k in range(PEERS):
        at = pl.ds(pl.multiple_of(((x[0] + k) & (PEERS - 1)) * step, 16), step)
        before = (one[at, :].astype(F32) + two[at, :].astype(F32)) * scale
        values = (0.5 * before * (1.0 + lax.erf(before * 0.7071067811865476))).astype(BF16)
        hidden[at, :] = values
        terms[k][:, :width] = dot_rows(values, flat(rows_mine), 1, 0).astype(BF16)
        terms[k][:, width:] = dot_rows(values, flat(rows_away), 1, 0).astype(BF16)


def fc1_kernel(features, x, one, two, three, four, tail_one, tail_two, rows_mine, rows_away, gain_mine, gain_away, *terms):
    step = terms[0].shape[0]
    width = rows_mine.shape[2]
    scale = scale_of(features, tail_one, tail_two, PEERS * step)
    for k in range(PEERS):
        at = pl.ds(pl.multiple_of(((x[0] + k) & (PEERS - 1)) * step, 16), step)
        before = (one[at, :].astype(F32) + two[at, :].astype(F32)) * scale
        slope = (three[at, :].astype(F32) + four[at, :].astype(F32)) * gelu_slope(before) * scale
        values = slope.astype(BF16)
        terms[k][:, :width] = (dot_rows(values, flat(rows_mine), 1, 0) * gain_mine[...]).astype(BF16)
        terms[k][:, width:] = (dot_rows(values, flat(rows_away), 1, 0) * gain_away[...]).astype(BF16)


def mix_kernel(hidden_0, hidden_1, w, out):
    cut = hidden_0.shape[0]
    total = dot_rows(hidden_0[...], w[: cut // TILE].reshape(cut, -1), 0, 0)
    total = total + dot_rows(hidden_1[...], w[cut // TILE :].reshape(-1, w.shape[2]), 0, 0)
    out[...] = total.astype(BF16).reshape(out.shape)


def local(kernel, out_shape, scalars, arrays):
    single = not isinstance(out_shape, list)
    return pl.pallas_call(
        kernel,
        out_shape=out_shape,
        in_specs=[SMEM] * len(scalars) + [VMEM] * len(arrays),
        out_specs=VMEM if single else [VMEM] * len(out_shape),
        cost_estimate=cost(1, 1),
        compiler_params=pltpu.CompilerParams(vmem_limit_bytes=40 * 1024 * 1024),
    )(*scalars, *arrays)


def column_picks(hidden, columns, layers):
    share = columns // 2
    picks = []
    for half in range(2):
        for low, high, padded in CHUNKS:
            for x in range(PEERS):
                for layer in range(layers):
                    part = np.zeros((padded, hidden), np.float32)
                    begin = layer * PEERS * columns + x * columns + half * share + low
                    part[np.arange(high - low), begin + np.arange(high - low)] = 1.0
                    picks.append(part)
    picks = np.concatenate(picks)
    return picks.reshape(2, picks.shape[0] // 2, hidden).astype(jnp.bfloat16)


def body(tiles, ln_gain, w_fc1, w_fc2, tile_count, embed_grad):
    replicas = lax.axis_size("dp")
    section = lax.axis_index("section")
    tensor = lax.axis_index("tensor")
    replica = lax.axis_index("dp")
    core = section % 2
    max_tiles, tile_rows, width_part = tiles.shape
    width = ln_gain.shape[0]
    hidden_part = w_fc1.shape[1]
    columns = hidden_part // replicas
    share = columns // 2
    layers = replicas // PEERS
    groups = max_tiles // PEERS
    rows = PEERS * TARGET_SLOTS * tile_rows
    block = jax.ShapeDtypeStruct((groups, tile_rows, width_part), BF16)
    pair = jax.ShapeDtypeStruct((2, groups, tile_rows, width_part), BF16)
    slots = jax.ShapeDtypeStruct((TARGET_SLOTS, tile_rows, width_part), BF16)
    full = jax.ShapeDtypeStruct((PEERS * TARGET_SLOTS, tile_rows, width_part), BF16)
    z_groups = [[z * PEERS + x for z in range(layers)] for x in range(PEERS)]
    counts = [PEERS * layers * padded for _, _, padded in CHUNKS]
    last = []

    def turn(x):
        if not last:
            return x
        x = after(x, *last)
        last[:] = last[-1:]
        return x

    def done(x):
        last.append(x)
        return x

    own_count = tile_count.reshape(1)
    place = jnp.stack([section, tensor]).astype(jnp.int32)
    x_place = (replica % PEERS).astype(jnp.int32).reshape(1)
    all_counts = [own_count] + [section_swap(own_count, m) for m in (1, 2, 3)]
    info = jnp.concatenate([place] + all_counts)
    gains = ln_gain.reshape(PEERS, width_part)
    gain_mine = lax.dynamic_index_in_dim(gains, section, 0)
    gain_away = lax.dynamic_index_in_dim(gains, section ^ 1, 0)
    picks = jnp.asarray(column_picks(hidden_part, columns, layers))

    def reordered(w, half, factor=None):
        count, size = picks.shape[1], width_part
        step = count // 4
        extra = [] if factor is None else [factor]
        return done(
            pl.pallas_call(
                reorder_kernel,
                grid_spec=pltpu.PrefetchScalarGridSpec(
                    num_scalar_prefetch=1,
                    grid=(count // step,),
                    in_specs=[
                        pl.BlockSpec((1, step, hidden_part), lambda i, half: (half[0], i, 0)),
                        pl.BlockSpec((size, hidden_part), lambda i, half: (0, 0)),
                    ]
                    + [pl.BlockSpec((1, size), lambda i, half: (0, 0)) for _ in extra],
                    out_specs=pl.BlockSpec((step // TILE, TILE, size), lambda i, half: (i, 0, 0)),
                ),
                out_shape=jax.ShapeDtypeStruct((count // TILE, TILE, size), BF16),
                cost_estimate=cost(1, 1),
                compiler_params=pltpu.CompilerParams(vmem_limit_bytes=40 * 1024 * 1024),
            )(half.reshape(1).astype(jnp.int32), picks, turn(w), *extra)
        )

    def spread_rows(own):
        near = [tensor_ring(own, k) for k in (1, 3)]
        return [own, near[0], tensor_ring(own, 2), near[1]]

    def join(pieces):
        return done(local(join_kernel, full, [place], [turn(pieces[0]), *pieces[1:]]))

    def project(c, w_mine, w_away, rows_mine, rows_away, extra=0):
        begin = sum(counts[:c])
        shape = jax.ShapeDtypeStruct((counts[c] + extra, rows), BF16)
        inputs = [w_mine, w_away, turn(rows_mine), rows_away]
        term = done(local(functools.partial(project_kernel, begin, counts[c]), shape, [], inputs))
        return term, section_swap(term, 2)

    def pieces_of(c):
        return [jax.ShapeDtypeStruct((counts[c] // PEERS, 2 * width_part), BF16)] * PEERS

    def over_x(terms):
        near = [x_ring(terms[k], k, replicas) for k in (1, 3)]
        return [terms[0], near[0], x_ring(terms[2], 2, replicas), near[1]]

    def tails(c):
        return list(sums[0]) if c == 0 else [x[counts[0] :] for x in sums[0]]

    def fence(pair):
        one, two = pair
        return one, done(turn(two))

    def make_fc2(c):
        one, two = sums[c]
        shape = [jax.ShapeDtypeStruct((counts[c], rows), BF16)] + pieces_of(c)
        two = turn(two)
        inputs = [one, two, *([one, two] if c == 0 else tails(c)), grad_mine, grad_away]
        values, *terms = local(functools.partial(fc2_kernel, width), shape, [x_place], inputs)
        done(terms[0])
        return values, over_x(terms)

    def make_fc1(c):
        one, two = sums[c]
        three, four = slopes_in[c]
        inputs = [one, two, three, turn(four), *tails(c), norm_mine, norm_away, gain_mine, gain_away]
        terms = local(functools.partial(fc1_kernel, width), pieces_of(c), [x_place], inputs)
        done(terms[0])
        return over_x(terms)

    def sum_x(c, got):
        total = done(sum(piece.astype(F32) for piece in [turn(got[0])] + got[1:]).astype(BF16))
        return total.reshape(layers, CHUNKS[c][2], 2 * width_part)

    def over_z(total):
        total = lax.all_to_all(total, "dp", 0, 0, axis_index_groups=z_groups, tiled=True)
        return jnp.sum(total.astype(F32), axis=0)

    def over_z_direct(total):
        z_place = replica // PEERS
        got = [lax.dynamic_index_in_dim(total, (z_place + k) % layers, 0, keepdims=False) for k in range(layers)]
        got = [got[0]] + [z_ring(got[k], k, replicas) for k in range(1, layers)]
        return sum(piece.astype(F32) for piece in got)

    def place_result(parts):
        total = jnp.concatenate(parts, axis=0)
        mine, away = total[:, :width_part], total[:, width_part:]
        away = section_swap(away, 1)
        whole = jnp.where(core == 0, jnp.concatenate([mine, away]), jnp.concatenate([away, mine]))
        return whole.T.reshape(width_part, 1, columns)

    sends = local(pack_kernel, [pair] * PEERS, [info], [tiles, embed_grad])
    done(sends[0])
    got = [dispatch(sends[k], k) for k in range(PEERS)]
    plan = pl.pallas_call(
        functools.partial(plan_kernel, groups),
        out_shape=jax.ShapeDtypeStruct((16,), jnp.int32),
        in_specs=[SMEM],
        out_specs=SMEM,
        cost_estimate=cost(1, 1),
    )(turn(info))
    up_away = section_swap(reordered(w_fc1, 1 - core, gain_mine), 1)
    up_mine = reordered(w_fc1, core, gain_mine)
    own_tiles, own_grads = local(compact_kernel, [slots, slots], [plan], [turn(got[0]), *got[1:]])
    done(own_tiles)
    down_away = section_swap(reordered(w_fc2, 1 - core), 1)
    down_mine = reordered(w_fc2, core)
    norm_pieces = spread_rows(own_tiles)
    norm_mine = join(norm_pieces)
    norm_away = section_swap(norm_mine, 1)
    sums = [project(0, up_mine, up_away, norm_mine, norm_away, TILE)]
    grad_pieces = spread_rows(after(own_grads, sums[0][0]))
    sums.append(project(1, up_mine, up_away, norm_mine, norm_away))
    sums[0] = fence(sums[0])
    grad_mine = join(grad_pieces)
    grad_away = section_swap(grad_mine, 1)
    hidden, parts_fc2, parts_fc1 = [None, None], [None, None], [None, None]
    slopes_in = [project(0, down_mine, down_away, grad_mine, grad_away)]
    sums[1] = fence(sums[1])
    hidden[0], parts_fc2[0] = make_fc2(0)
    slopes_in.append(project(1, down_mine, down_away, grad_mine, grad_away))
    done(parts_fc2[0][1])
    done(parts_fc2[0][3])
    slopes_in[0] = fence(slopes_in[0])
    hidden[1], parts_fc2[1] = make_fc2(1)
    parts_fc1[0] = make_fc1(0)
    sum_a = sum_x(0, parts_fc2[0])
    slopes_in[1] = fence(slopes_in[1])
    parts_fc1[1] = make_fc1(1)

    def mix(w):
        return done(local(mix_kernel, full, [], [turn(hidden[0]), hidden[1], w]))

    mix_away = section_swap(mix(down_away), 1)
    mixed = mix(down_mine)
    mixed = done((turn(mixed).astype(F32) + mix_away.astype(F32)).astype(BF16))
    mixed = lax.all_to_all(mixed, "tensor", 0, 0, tiled=True).reshape((PEERS,) + slots.shape)
    sum_b = sum_x(1, parts_fc2[1])
    done(mixed)
    total = over_z(turn(jnp.concatenate([sum_a, sum_b], axis=1)))
    sum_a = sum_x(0, parts_fc1[0])
    spread = local(expand_kernel, [block] * PEERS, [plan], [turn(mixed)])
    done(spread[0])
    back = [give_back(spread[k], k) for k in range(PEERS)]
    sum_b = sum_x(1, parts_fc1[1])
    done(total)
    part_a = over_z(turn(sum_a))
    part_b = over_z_direct(sum_b)
    embeds = local(finish_kernel, jax.ShapeDtypeStruct(tiles.shape, BF16), [plan], [turn(tiles), *back])
    done(embeds)
    cut = CHUNKS[0][2]
    left = share - cut
    final_fc2 = [total[:cut], total[cut : cut + left]]
    final_fc1 = [turn(part_a), part_b[:left]]
    return (embeds, place_result(final_fc1), place_result(final_fc2))


def solution(mesh):
    placed = (
        P(("dp", "section"), None, "tensor"),
        P(),
        P("section", "tensor"),
        P("section", "tensor"),
        P("dp", "section"),
        P(("dp", "section"), None, "tensor"),
    )
    return jax.shard_map(
        body,
        mesh=mesh,
        in_specs=placed,
        out_specs=(
            P(("dp", "section"), None, "tensor"),
            P("section", "tensor", "dp"),
            P("section", "tensor", "dp"),
        ),
        check_vma=False,
    )
```

```python
import functools

import jax
import jax.numpy as jnp
import numpy as np
from jax import lax
from jax.experimental import pallas as pl
from jax.experimental.pallas import tpu as pltpu
from jax.sharding import PartitionSpec as P

epsilon = 1e-06
F32 = jnp.float32
BF16 = jnp.bfloat16
PEERS = 4
TARGET_SLOTS = 6
TILE = 16
CHUNKS = ((0, 32, 32), (32, 50, 20))
VMEM = pl.BlockSpec(memory_space=pltpu.VMEM)
SMEM = pl.BlockSpec(memory_space=pltpu.SMEM)


def gelu_slope(values):
    normal_cdf = 0.5 * (1.0 + lax.erf(values * 0.7071067811865476))
    return normal_cdf + values * jnp.exp(-0.5 * values * values) * 0.3989422804014327


def section_swap(x, mask):
    return lax.ppermute(x, "section", [(s, s ^ mask) for s in range(PEERS)])


def tensor_ring(x, step):
    return lax.ppermute(x, "tensor", [(t, (t + step) % PEERS) for t in range(PEERS)])


def x_ring(x, step, replicas):
    pairs = [(d, d - d % PEERS + (d % PEERS + step) % PEERS) for d in range(replicas)]
    return lax.ppermute(x, "dp", pairs)


def z_ring(x, step, replicas):
    pairs = [(d, (d + step * PEERS) % replicas) for d in range(replicas)]
    return lax.ppermute(x, "dp", pairs)


def dispatch(x, step):
    pairs = [(i * PEERS + f, f * PEERS + (i + step) % PEERS) for i in range(PEERS) for f in range(PEERS)]
    return lax.ppermute(x, ("section", "tensor"), pairs)


def give_back(x, step):
    pairs = [(f * PEERS + (i + step) % PEERS, i * PEERS + f) for i in range(PEERS) for f in range(PEERS)]
    return lax.ppermute(x, ("section", "tensor"), pairs)


def cost(flops, moved):
    return pl.CostEstimate(flops=flops, bytes_accessed=moved, transcendentals=0)


def after(x, *others):
    return lax.optimization_barrier((x,) + others)[0]


def choose(values, index):
    chosen = values[0]
    for i in range(1, len(values)):
        chosen = jnp.where(index == i, values[i], chosen)
    return chosen


def read_counts(info):
    section = info[0]
    counts = [choose([info[2 + m] for m in range(PEERS)], section ^ i) for i in range(PEERS)]
    offsets = [jnp.int32(0)]
    for i in range(PEERS - 1):
        offsets.append(offsets[-1] + counts[i])
    return counts, offsets


def first_of(info, offsets, k):
    section = info[0]
    return (section + k - choose(offsets, section)) & (PEERS - 1)


def plan_kernel(groups, info, out):
    counts, offsets = read_counts(info)
    tensor = info[1]
    out[3 * PEERS] = info[2]
    for k in range(PEERS):
        out[k] = first_of(info, offsets, k)
        source = (tensor - k) & (PEERS - 1)
        offset = choose(offsets, source)
        first = (tensor - offset) & (PEERS - 1)
        out[PEERS + k] = (offset + first) >> 2
        live = (choose(counts, source) - first + PEERS - 1) >> 2
        out[2 * PEERS + k] = jnp.minimum(jnp.maximum(live, 0), groups)


def pack_kernel(info, tiles, grads, *sends):
    _, offsets = read_counts(info)
    for k in range(PEERS):
        first = first_of(info, offsets, k)
        for p in range(sends[k].shape[1]):
            sends[k][0, p] = tiles[first + PEERS * p]
            sends[k][1, p] = grads[first + PEERS * p]


def compact_kernel(plan, g0, g1, g2, g3, tiles, grads):
    for k, got in enumerate((g0, g1, g2, g3)):
        for p in range(got.shape[1]):

            @pl.when(p < plan[2 * PEERS + k])
            def _():
                slot = plan[PEERS + k] + p
                tiles[slot] = got[0, p]
                grads[slot] = got[1, p]


def join_kernel(place, p0, p1, p2, p3, out):
    size = p0.shape[0]
    for k, piece in enumerate((p0, p1, p2, p3)):
        out[pl.ds(((place[1] - k) & (PEERS - 1)) * size, size)] = piece[...]


def expand_kernel(plan, mixed, *outs):
    for k in range(PEERS):
        for p in range(outs[k].shape[0]):
            slot = jnp.minimum(plan[PEERS + k] + p, TARGET_SLOTS - 1)
            total = mixed[0, slot].astype(F32) + mixed[1, slot].astype(F32)
            total = total + mixed[2, slot].astype(F32) + mixed[3, slot].astype(F32)
            outs[k][p] = total.astype(BF16)


def finish_kernel(plan, tiles, b0, b1, b2, b3, out):
    for k, back in enumerate((b0, b1, b2, b3)):
        for p in range(back.shape[0]):
            j = plan[k] + PEERS * p
            total = (tiles[j].astype(F32) + back[p].astype(F32)).astype(BF16)
            out[j] = jnp.where(j < plan[3 * PEERS], total, jnp.zeros_like(total))


def dot_rows(left, right, left_axis, right_axis):
    return lax.dot_general(left, right, (((left_axis,), (right_axis,)), ((), ())), preferred_element_type=F32)


def flat(ref):
    return ref[...].reshape(ref.shape[0] * ref.shape[1], ref.shape[2])


def reorder_kernel(half, pick, w, *rest):
    factor, out = rest if len(rest) == 2 else (None, rest[0])
    part = dot_rows(pick[0], w[...], 1, 1)
    if factor is not None:
        part = part * factor[...]
    out[...] = part.astype(BF16).reshape(out.shape)


def row_squares(rows):
    values = flat(rows).astype(F32)
    values = values * values
    high = values.astype(BF16)
    low = (values - high.astype(F32)).astype(BF16)
    ones = jnp.ones((TILE, values.shape[1]), BF16)
    return dot_rows(ones, high, 1, 1) + dot_rows(ones, low, 1, 1)


def project_kernel(begin, count, w_mine, w_away, rows_mine, rows_away, out):
    step = count // PEERS
    if out.shape[0] > count:
        squares = row_squares(rows_mine) + row_squares(rows_away)
        high = squares.astype(BF16)
        rest = squares - high.astype(F32)
        middle = rest.astype(BF16)
        low = (rest - middle.astype(F32)).astype(BF16)
        spot = lax.broadcasted_iota(jnp.int32, squares.shape, 0)
        part = jnp.where(spot == 0, high.astype(F32), jnp.where(spot == 1, middle.astype(F32), low.astype(F32)))
        out[count:, :] = jnp.where(spot < 3, part, 0.0).astype(BF16)

    def piece(i, carry):
        at = pl.ds((begin + i * step) // TILE, step // TILE)
        mine = w_mine[at].reshape(step, w_mine.shape[2])
        away = w_away[at].reshape(step, w_away.shape[2])
        total = dot_rows(mine, flat(rows_mine), 1, 1) + dot_rows(away, flat(rows_away), 1, 1)
        out[pl.ds(pl.multiple_of(i * step, TILE), step), :] = total.astype(BF16)
        return carry

    lax.fori_loop(0, PEERS, piece, 0)


def scale_of(width, one, two, count):
    if one.shape[0] > count:
        one, two = one.at[pl.ds(count, TILE), :], two.at[pl.ds(count, TILE), :]
    both = one[...].astype(F32) + two[...].astype(F32)
    return lax.rsqrt(jnp.sum(both, axis=0, keepdims=True) * (1.0 / width) + epsilon)


def fc2_kernel(features, x, one, two, tail_one, tail_two, rows_mine, rows_away, hidden, *terms):
    step = terms[0].shape[0]
    width = rows_mine.shape[2]
    scale = scale_of(features, tail_one, tail_two, PEERS * step)
    for k in range(PEERS):
        at = pl.ds(pl.multiple_of(((x[0] + k) & (PEERS - 1)) * step, 16), step)
        before = (one[at, :].astype(F32) + two[at, :].astype(F32)) * scale
        values = (0.5 * before * (1.0 + lax.erf(before * 0.7071067811865476))).astype(BF16)
        hidden[at, :] = values
        terms[k][:, :width] = dot_rows(values, flat(rows_mine), 1, 0).astype(BF16)
        terms[k][:, width:] = dot_rows(values, flat(rows_away), 1, 0).astype(BF16)


def fc1_kernel(features, x, one, two, three, four, tail_one, tail_two, rows_mine, rows_away, gain_mine, gain_away, *terms):
    step = terms[0].shape[0]
    width = rows_mine.shape[2]
    scale = scale_of(features, tail_one, tail_two, PEERS * step)
    for k in range(PEERS):
        at = pl.ds(pl.multiple_of(((x[0] + k) & (PEERS - 1)) * step, 16), step)
        before = (one[at, :].astype(F32) + two[at, :].astype(F32)) * scale
        slope = (three[at, :].astype(F32) + four[at, :].astype(F32)) * gelu_slope(before) * scale
        values = slope.astype(BF16)
        terms[k][:, :width] = (dot_rows(values, flat(rows_mine), 1, 0) * gain_mine[...]).astype(BF16)
        terms[k][:, width:] = (dot_rows(values, flat(rows_away), 1, 0) * gain_away[...]).astype(BF16)


def mix_kernel(hidden_0, hidden_1, w, out):
    cut = hidden_0.shape[0]
    total = dot_rows(hidden_0[...], w[: cut // TILE].reshape(cut, -1), 0, 0)
    total = total + dot_rows(hidden_1[...], w[cut // TILE :].reshape(-1, w.shape[2]), 0, 0)
    out[...] = total.astype(BF16).reshape(out.shape)


def local(kernel, out_shape, scalars, arrays):
    single = not isinstance(out_shape, list)
    return pl.pallas_call(
        kernel,
        out_shape=out_shape,
        in_specs=[SMEM] * len(scalars) + [VMEM] * len(arrays),
        out_specs=VMEM if single else [VMEM] * len(out_shape),
        cost_estimate=cost(1, 1),
        compiler_params=pltpu.CompilerParams(vmem_limit_bytes=40 * 1024 * 1024),
    )(*scalars, *arrays)


def column_picks(hidden, columns, layers):
    share = columns // 2
    picks = []
    for half in range(2):
        for low, high, padded in CHUNKS:
            for x in range(PEERS):
                for layer in range(layers):
                    part = np.zeros((padded, hidden), np.float32)
                    begin = layer * PEERS * columns + x * columns + half * share + low
                    part[np.arange(high - low), begin + np.arange(high - low)] = 1.0
                    picks.append(part)
    picks = np.concatenate(picks)
    return picks.reshape(2, picks.shape[0] // 2, hidden).astype(jnp.bfloat16)


def body(tiles, ln_gain, w_fc1, w_fc2, tile_count, embed_grad):
    replicas = lax.axis_size("dp")
    section = lax.axis_index("section")
    tensor = lax.axis_index("tensor")
    replica = lax.axis_index("dp")
    core = section % 2
    max_tiles, tile_rows, width_part = tiles.shape
    width = ln_gain.shape[0]
    hidden_part = w_fc1.shape[1]
    columns = hidden_part // replicas
    share = columns // 2
    layers = replicas // PEERS
    groups = max_tiles // PEERS
    rows = PEERS * TARGET_SLOTS * tile_rows
    block = jax.ShapeDtypeStruct((groups, tile_rows, width_part), BF16)
    pair = jax.ShapeDtypeStruct((2, groups, tile_rows, width_part), BF16)
    slots = jax.ShapeDtypeStruct((TARGET_SLOTS, tile_rows, width_part), BF16)
    full = jax.ShapeDtypeStruct((PEERS * TARGET_SLOTS, tile_rows, width_part), BF16)
    z_groups = [[z * PEERS + x for z in range(layers)] for x in range(PEERS)]
    counts = [PEERS * layers * padded for _, _, padded in CHUNKS]
    last = []

    def turn(x):
        if not last:
            return x
        x = after(x, *last)
        last[:] = last[-1:]
        return x

    def done(x):
        last.append(x)
        return x

    own_count = tile_count.reshape(1)
    place = jnp.stack([section, tensor]).astype(jnp.int32)
    x_place = (replica % PEERS).astype(jnp.int32).reshape(1)
    all_counts = [own_count] + [section_swap(own_count, m) for m in (1, 2, 3)]
    info = jnp.concatenate([place] + all_counts)
    gains = ln_gain.reshape(PEERS, width_part)
    gain_mine = lax.dynamic_index_in_dim(gains, section, 0)
    gain_away = lax.dynamic_index_in_dim(gains, section ^ 1, 0)
    picks = jnp.asarray(column_picks(hidden_part, columns, layers))

    def reordered(w, half, factor=None):
        count, size = picks.shape[1], width_part
        step = count // 4
        extra = [] if factor is None else [factor]
        return done(
            pl.pallas_call(
                reorder_kernel,
                grid_spec=pltpu.PrefetchScalarGridSpec(
                    num_scalar_prefetch=1,
                    grid=(count // step,),
                    in_specs=[
                        pl.BlockSpec((1, step, hidden_part), lambda i, half: (half[0], i, 0)),
                        pl.BlockSpec((size, hidden_part), lambda i, half: (0, 0)),
                    ]
                    + [pl.BlockSpec((1, size), lambda i, half: (0, 0)) for _ in extra],
                    out_specs=pl.BlockSpec((step // TILE, TILE, size), lambda i, half: (i, 0, 0)),
                ),
                out_shape=jax.ShapeDtypeStruct((count // TILE, TILE, size), BF16),
                cost_estimate=cost(1, 1),
                compiler_params=pltpu.CompilerParams(vmem_limit_bytes=40 * 1024 * 1024),
            )(half.reshape(1).astype(jnp.int32), picks, turn(w), *extra)
        )

    def spread_rows(own):
        near = [tensor_ring(own, k) for k in (1, 3)]
        return [own, near[0], tensor_ring(own, 2), near[1]]

    def join(pieces):
        return done(local(join_kernel, full, [place], [turn(pieces[0]), *pieces[1:]]))

    def project(c, w_mine, w_away, rows_mine, rows_away, extra=0):
        begin = sum(counts[:c])
        shape = jax.ShapeDtypeStruct((counts[c] + extra, rows), BF16)
        inputs = [w_mine, w_away, turn(rows_mine), rows_away]
        term = done(local(functools.partial(project_kernel, begin, counts[c]), shape, [], inputs))
        return term, section_swap(term, 2)

    def pieces_of(c):
        return [jax.ShapeDtypeStruct((counts[c] // PEERS, 2 * width_part), BF16)] * PEERS

    def over_x(terms):
        near = [x_ring(terms[k], k, replicas) for k in (1, 3)]
        return [terms[0], near[0], x_ring(terms[2], 2, replicas), near[1]]

    def tails(c):
        return list(sums[0]) if c == 0 else [x[counts[0] :] for x in sums[0]]

    def fence(pair):
        one, two = pair
        return one, done(turn(two))

    def make_fc2(c):
        one, two = sums[c]
        shape = [jax.ShapeDtypeStruct((counts[c], rows), BF16)] + pieces_of(c)
        two = turn(two)
        inputs = [one, two, *([one, two] if c == 0 else tails(c)), grad_mine, grad_away]
        values, *terms = local(functools.partial(fc2_kernel, width), shape, [x_place], inputs)
        done(terms[0])
        return values, over_x(terms)

    def make_fc1(c):
        one, two = sums[c]
        three, four = slopes_in[c]
        inputs = [one, two, three, turn(four), *tails(c), norm_mine, norm_away, gain_mine, gain_away]
        terms = local(functools.partial(fc1_kernel, width), pieces_of(c), [x_place], inputs)
        done(terms[0])
        return over_x(terms)

    def sum_x(c, got):
        total = done(sum(piece.astype(F32) for piece in [turn(got[0])] + got[1:]).astype(BF16))
        return total.reshape(layers, CHUNKS[c][2], 2 * width_part)

    def over_z(total):
        total = lax.all_to_all(total, "dp", 0, 0, axis_index_groups=z_groups, tiled=True)
        return jnp.sum(total.astype(F32), axis=0)

    def over_z_direct(total):
        z_place = replica // PEERS
        got = [lax.dynamic_index_in_dim(total, (z_place + k) % layers, 0, keepdims=False) for k in range(layers)]
        got = [got[0]] + [z_ring(got[k], k, replicas) for k in range(1, layers)]
        return sum(piece.astype(F32) for piece in got)

    def place_result(parts):
        total = jnp.concatenate(parts, axis=0)
        mine, away = total[:, :width_part], total[:, width_part:]
        away = section_swap(away, 1)
        whole = jnp.where(core == 0, jnp.concatenate([mine, away]), jnp.concatenate([away, mine]))
        return whole.T.reshape(width_part, 1, columns)

    sends = local(pack_kernel, [pair] * PEERS, [info], [tiles, embed_grad])
    done(sends[0])
    got = [dispatch(sends[k], k) for k in range(PEERS)]
    plan = pl.pallas_call(
        functools.partial(plan_kernel, groups),
        out_shape=jax.ShapeDtypeStruct((16,), jnp.int32),
        in_specs=[SMEM],
        out_specs=SMEM,
        cost_estimate=cost(1, 1),
    )(turn(info))
    up_away = section_swap(reordered(w_fc1, 1 - core, gain_mine), 1)
    up_mine = reordered(w_fc1, core, gain_mine)
    own_tiles, own_grads = local(compact_kernel, [slots, slots], [plan], [turn(got[0]), *got[1:]])
    done(own_tiles)
    down_away = section_swap(reordered(w_fc2, 1 - core), 1)
    down_mine = reordered(w_fc2, core)
    norm_pieces = spread_rows(own_tiles)
    norm_mine = join(norm_pieces)
    norm_away = section_swap(norm_mine, 1)
    sums = [project(0, up_mine, up_away, norm_mine, norm_away, TILE)]
    grad_pieces = spread_rows(after(own_grads, sums[0][0]))
    sums.append(project(1, up_mine, up_away, norm_mine, norm_away))
    sums[0] = fence(sums[0])
    grad_mine = join(grad_pieces)
    grad_away = section_swap(grad_mine, 1)
    hidden, parts_fc2, parts_fc1 = [None, None], [None, None], [None, None]
    slopes_in = [project(0, down_mine, down_away, grad_mine, grad_away)]
    sums[1] = fence(sums[1])
    hidden[0], parts_fc2[0] = make_fc2(0)
    slopes_in.append(project(1, down_mine, down_away, grad_mine, grad_away))
    slopes_in[0] = fence(slopes_in[0])
    hidden[1], parts_fc2[1] = make_fc2(1)
    done(parts_fc2[0][1])
    done(parts_fc2[0][3])
    parts_fc1[0] = make_fc1(0)
    sum_a = sum_x(0, parts_fc2[0])
    slopes_in[1] = fence(slopes_in[1])
    parts_fc1[1] = make_fc1(1)

    def mix(w):
        return done(local(mix_kernel, full, [], [turn(hidden[0]), hidden[1], w]))

    mix_away = section_swap(mix(down_away), 1)
    mixed = mix(down_mine)
    mixed = done((turn(mixed).astype(F32) + mix_away.astype(F32)).astype(BF16))
    mixed = lax.all_to_all(mixed, "tensor", 0, 0, tiled=True).reshape((PEERS,) + slots.shape)
    sum_b = sum_x(1, parts_fc2[1])
    done(mixed)
    total = over_z(turn(jnp.concatenate([sum_a, sum_b], axis=1)))
    sum_a = sum_x(0, parts_fc1[0])
    spread = local(expand_kernel, [block] * PEERS, [plan], [turn(mixed)])
    done(spread[0])
    back = [give_back(spread[k], k) for k in range(PEERS)]
    sum_b = sum_x(1, parts_fc1[1])
    done(total)
    part_a = over_z(turn(sum_a))
    part_b = over_z_direct(sum_b)
    embeds = local(finish_kernel, jax.ShapeDtypeStruct(tiles.shape, BF16), [plan], [turn(tiles), *back])
    done(embeds)
    cut = CHUNKS[0][2]
    left = share - cut
    final_fc2 = [total[:cut], total[cut : cut + left]]
    final_fc1 = [turn(part_a), part_b[:left]]
    return (embeds, place_result(final_fc1), place_result(final_fc2))


def solution(mesh):
    placed = (
        P(("dp", "section"), None, "tensor"),
        P(),
        P("section", "tensor"),
        P("section", "tensor"),
        P("dp", "section"),
        P(("dp", "section"), None, "tensor"),
    )
    return jax.shard_map(
        body,
        mesh=mesh,
        in_specs=placed,
        out_specs=(
            P(("dp", "section"), None, "tensor"),
            P("section", "tensor", "dp"),
            P("section", "tensor", "dp"),
        ),
        check_vma=False,
    )
```
